256 devices in a mesh: row: 16 (over y, z_hi, core), col: 16 (over z_lo, x).
Axes of the slice: x: 4, y: 4, z: 8 (z_hi: 2, z_lo: 4; z = z_hi * 4 + z_lo), core: 2. Of those that a mesh axis runs over, the one named last changes fastest.
Arguments:
- iterate: float32 [5120, 12800], P('row', 'col'), may hold values from -0.03125 to 0.03125
Outputs:
- update: float32 [5120, 12800], P('row', 'col')
The draws below stay inside these ranges and needn't reach their ends.
All inputs are finite; a program needn't handle non-finite values.
Results may differ from the reference program's by a relative error of at most 0.0043.
Values may be sent and summed in bfloat16 or wider, within the bound.
No kernel may reach another device: no remote copies, remote signals or barrier semaphores. Data moves between devices by JAX's collectives and lax.ppermute only.
A program may use at most 128 MiB of HBM per device.

```python
import math
import jax
import jax.numpy as jnp
from jax import lax

M = 5120
N = 12800


def block_scale(stream_key, shape, cuts, least, largest):
    level, own = 1.0, jax.random.fold_in(stream_key, 6)
    for position, blocks in cuts:
        steps = jnp.exp(jax.random.uniform(jax.random.fold_in(own, position), (blocks,), jnp.float32, least / len(cuts), largest / len(cuts)))
        level = level * jnp.repeat(steps, shape[position] // blocks).reshape([-1 if axis == position else 1 for axis in range(len(shape))])
    return level


def noise(stream_key, extent, spread, limit, cuts=(), dtype=jnp.bfloat16):
    entries = spread * jax.random.normal(stream_key, extent, jnp.float32)
    if cuts:
        entries = entries * block_scale(stream_key, extent, cuts, -0.22, 0.18)
    return jnp.clip(entries, -limit, limit).astype(dtype)


def setup_inputs(seed: int = 0) -> dict:
    key_list = jax.random.split(jax.random.key(seed), 2)
    iterate = noise(key_list[0], (M, N), (3 * N) ** -0.5, 0.03125, ((0, 16), (1, 16)), jnp.float32)
    return dict(iterate=iterate)


coef_a = 3.4445
coef_b = -4.775
coef_c = 2.0315

def reference(iterate):
    narrow = iterate.astype(jnp.bfloat16)
    gram = lax.dot_general(narrow, narrow, (((1,), (1,)), ((), ())), preferred_element_type=jnp.float32)
    gram = lax.optimization_barrier(gram.astype(jnp.bfloat16))
    square = jnp.dot(gram, gram, preferred_element_type=jnp.float32)
    mixing = (coef_b * gram.astype(jnp.float32) + coef_c * square).astype(jnp.bfloat16)
    product = jnp.dot(mixing, narrow, preferred_element_type=jnp.float32)
    factor = 0.2 * math.sqrt(max(M, N))
    return factor * (coef_a * iterate + product)
```

```python
import math

import jax
import jax.numpy as jnp
from jax import lax
from jax.sharding import PartitionSpec as P

coef_a = 3.4445
coef_b = -4.775
coef_c = 2.0315

axes = ("row", "col")


def fetch(value, source):
    pairs = []
    for row in range(16):
        for col in range(16):
            y, half, core, run, x = source(row // 4, row // 2 % 2, row % 2, col // 4, col % 4)
            pairs.append((((y * 2 + half) * 2 + core) * 16 + run * 4 + x, row * 16 + col))
    return lax.ppermute(value, axes, pairs)


def other_core(value):
    return fetch(value, lambda y, half, core, run, x: (y, half, 1 - core, run, x))


def other_half(value):
    return fetch(value, lambda y, half, core, run, x: (y, 1 - half, core, run, x))


def along_y(value, step):
    return fetch(value, lambda y, half, core, run, x: (y ^ x ^ step, half, core, run, x))


def along_run(value, step):
    return fetch(value, lambda y, half, core, run, x: (y, half, core, run ^ step, x))


def along_x(value, step):
    return fetch(value, lambda y, half, core, run, x: (y, half, core, run, x ^ step))


def gather_rows(block):
    found = {}
    for far, value in enumerate((block, other_half(block))):
        for step in range(4):
            found[step, far] = along_y(value, step)
    return found


def times(left, right):
    return jnp.dot(left, right, preferred_element_type=jnp.float32)


def times_transposed(left, right):
    return lax.dot_general(
        left, right, (((1,), (1,)), ((), ())), preferred_element_type=jnp.float32
    )


def total(values):
    summed = values[0].astype(jnp.float32)
    for value in values[1:]:
        summed = summed + value.astype(jnp.float32)
    return summed


def picked(stacked, index, rows):
    return lax.dynamic_slice_in_dim(stacked, index * rows, rows, 0)


def local(iterate):
    rows = iterate.shape[0]
    run = lax.axis_index("col") // 4
    total_rows = rows * lax.axis_size("row")
    total_cols = iterate.shape[1] * lax.axis_size("col")
    narrow = iterate.astype(jnp.bfloat16)
    chip_rows = jnp.concatenate([narrow, other_core(narrow)], axis=0)
    blocks = gather_rows(narrow)

    reduced = []
    for far in range(2):
        parts = []
        for step in range(4):
            part = times_transposed(chip_rows, blocks[step, far]).astype(jnp.bfloat16)
            parts.append(along_x(part, step) if step else part)
        reduced.append(total(parts).astype(jnp.bfloat16))
    reduced = jnp.concatenate(reduced, axis=0)
    parts = [picked(reduced, run ^ step, rows) for step in range(4)]
    tile = total([along_run(part, step) if step else part for step, part in enumerate(parts)])
    tile = tile.astype(jnp.bfloat16)

    tiles = jnp.concatenate(
        [along_run(tile, step) if step else tile for step in range(4)], axis=0
    )
    gram = {}
    for far in range(2):
        chunk = jnp.concatenate(
            [picked(tiles, run ^ (2 * far + core), rows) for core in range(2)], axis=0
        )
        for step in range(4):
            gram[step, far] = along_x(chunk, step) if step else chunk

    def multiplied(right):
        product = total([times(gram[key], right[key]) for key in gram])
        return product[:rows] + other_core(product[rows:].astype(jnp.bfloat16)).astype(jnp.float32)

    inner = coef_b * narrow.astype(jnp.float32) + coef_c * multiplied(blocks)
    product = multiplied(gather_rows(inner.astype(jnp.bfloat16)))
    factor = 0.2 * math.sqrt(max(total_rows, total_cols))
    return factor * (coef_a * iterate + product)


def solution(mesh):
    placed = (P("row", "col"),)
    return jax.shard_map(
        local, mesh=mesh, in_specs=placed, out_specs=P("row", "col"), check_vma=False
    )
```

```python
import math

import jax
import jax.numpy as jnp
from jax import lax
from jax.sharding import PartitionSpec as P

coef_a = 3.4445
coef_b = -4.775
coef_c = 2.0315

axes = ("row", "col")


def fetch(value, source):
    pairs = []
    for row in range(16):
        for col in range(16):
            y, half, core, run, x = source(row // 4, row // 2 % 2, row % 2, col // 4, col % 4)
            pairs.append((((y * 2 + half) * 2 + core) * 16 + run * 4 + x, row * 16 + col))
    return lax.ppermute(value, axes, pairs)


def other_core(value):
    return fetch(value, lambda y, half, core, run, x: (y, half, 1 - core, run, x))


def other_half(value):
    return fetch(value, lambda y, half, core, run, x: (y, 1 - half, core, run, x))


def toward_y(step):
    return lambda y, half, core, run, x: ((y + step) % 4, half, core, run, x)


def toward_x(step):
    return lambda y, half, core, run, x: (y, half, core, run, (x + step) % 4)


def neighbours(value, toward):
    return fetch(value, toward(1)), fetch(value, toward(-1))


def opposite(found, toward, axis):
    size = found[0].shape[axis] // 2
    return (
        fetch(lax.slice_in_dim(found[0], 0, size, axis=axis), toward(1)),
        fetch(lax.slice_in_dim(found[1], size, 2 * size, axis=axis), toward(-1)),
    )


def around(value, found, halves, axis):
    return jnp.concatenate([value, found[0], jnp.concatenate(halves, axis=axis), found[1]])


ordered = lax.optimization_barrier


def gather_rows(value):
    found, far = neighbours(value, toward_y), other_half(value)
    halves, far = ordered((opposite(found, toward_y, 0), far))
    far_found = neighbours(far, toward_y)
    far_halves = opposite(far_found, toward_y, 0)
    return [around(value, found, halves, 0), around(far, far_found, far_halves, 0)]


def along_run(values):
    return [values[0]] + [
        fetch(values[step], lambda y, half, core, run, x, step=step: (y, half, core, run ^ step, x))
        for step in range(1, 4)
    ]


def along_x(values):
    return [values[0]] + [
        fetch(
            values[step],
            lambda y, half, core, run, x, step=step: (y, half, core, run, (x - step) % 4),
        )
        for step in range(1, 4)
    ]


def times(left, right):
    return jnp.dot(left, right, preferred_element_type=jnp.float32)


def times_transposed(left, right):
    return lax.dot_general(
        left, right, (((1,), (1,)), ((), ())), preferred_element_type=jnp.float32
    )


def total(values):
    summed = values[0].astype(jnp.float32)
    for value in values[1:]:
        summed = summed + value.astype(jnp.float32)
    return summed


def quarters(value):
    rows, cols = (size // 2 for size in value.shape)
    return [value[i * rows : (i + 1) * rows, j * cols : (j + 1) * cols] for j in range(2) for i in range(2)]


def swapped(parts, index):
    for bit in (1, 2):
        on = (index & bit) != 0
        parts = [jnp.where(on, parts[i ^ bit], parts[i]) for i in range(4)]
    return parts


def rolled(stacked, index):
    size = stacked.shape[0] // 4
    parts = [stacked[i * size : (i + 1) * size] for i in range(4)]
    for bit in (1, 2):
        on = (index & bit) != 0
        parts = [jnp.where(on, parts[(i + bit) % 4], parts[i]) for i in range(4)]
    return jnp.concatenate(parts)


def scattered_x(left, right):
    partial = times_transposed(left, right).astype(jnp.bfloat16)
    size = partial.shape[0] // 4
    return along_x([partial[i * size : (i + 1) * size] for i in range(4)])


def scattered_run(parts, run):
    return along_run(swapped(quarters(total(parts).astype(jnp.bfloat16)), run))


def gathered_run(parts):
    return along_run([total(parts).astype(jnp.bfloat16)] * 4)


def strip_of(tiles, run):
    tiles = swapped(tiles, run)
    return jnp.concatenate([jnp.concatenate(tiles[:2]), jnp.concatenate(tiles[2:])], axis=1)


def multiplied(grams, rights):
    rows = grams[0].shape[0] // 2
    other = total([times(gram[rows:], right) for gram, right in zip(grams, rights)])
    own = total([times(gram[:rows], right) for gram, right in zip(grams, rights)])
    return own + other_core(other.astype(jnp.bfloat16)).astype(jnp.float32)


def local(iterate):
    run = lax.axis_index("col") // 4
    x = lax.axis_index("col") % 4
    total_rows = iterate.shape[0] * lax.axis_size("row")
    total_cols = iterate.shape[1] * lax.axis_size("col")
    narrow = iterate.astype(jnp.bfloat16)
    left = rolled(jnp.concatenate([narrow, other_core(narrow)]), x)

    found, far = neighbours(narrow, toward_y), other_half(narrow)
    halves, far = ordered((opposite(found, toward_y, 0), far))
    columns = [around(narrow, found, halves, 0)]
    found = neighbours(far, toward_y)
    near_parts = scattered_x(left, columns[0])
    halves, near_parts = ordered((opposite(found, toward_y, 0), near_parts))
    columns.append(around(far, found, halves, 0))

    far_parts = scattered_x(left, columns[1])
    tiles = gathered_run(scattered_run(near_parts, run))
    tiles, far_parts = ordered((tiles, far_parts))
    near_strip = strip_of(tiles, run)
    found, parts = ordered((neighbours(near_strip, toward_x), scattered_run(far_parts, run)))
    halves, tiles = ordered((opposite(found, toward_x, 1), gathered_run(parts)))
    near_gram = rolled(around(near_strip, found, halves, 1), -x)
    far_strip = strip_of(tiles, run)
    found = neighbours(far_strip, toward_x)
    halves = opposite(found, toward_x, 1)
    grams = [near_gram, rolled(around(far_strip, found, halves, 1), -x)]

    inner = coef_b * narrow.astype(jnp.float32) + coef_c * multiplied(grams, columns)
    product = multiplied(grams, gather_rows(inner.astype(jnp.bfloat16)))
    factor = 0.2 * math.sqrt(max(total_rows, total_cols))
    return factor * (coef_a * iterate + product)


def solution(mesh):
    placed = (P("row", "col"),)
    return jax.shard_map(
        local, mesh=mesh, in_specs=placed, out_specs=P("row", "col"), check_vma=False
    )
```

```python
import functools
import math

import jax
import jax.numpy as jnp
from jax import lax
from jax.experimental import pallas as pl
from jax.experimental.pallas import tpu as pltpu
from jax.sharding import PartitionSpec as P

coef_a = 3.4445
coef_b = -4.775
coef_c = 2.0315

axes = ("row", "col")
ordered = lax.optimization_barrier


def fetch(value, source):
    pairs = []
    for row in range(16):
        for col in range(16):
            y, half, core, run, x = source(row // 4, row // 2 % 2, row % 2, col // 4, col % 4)
            pairs.append((((y * 2 + half) * 2 + core) * 16 + run * 4 + x, row * 16 + col))
    return lax.ppermute(value, axes, pairs)


def other_core(value):
    return fetch(value, lambda y, half, core, run, x: (y, half, 1 - core, run, x))


def other_half(value):
    return fetch(value, lambda y, half, core, run, x: (y, 1 - half, core, run, x))


def toward_y(step):
    return lambda y, half, core, run, x: ((y + step) % 4, half, core, run, x)


def toward_x(step):
    return lambda y, half, core, run, x: (y, half, core, run, (x + step) % 4)


def neighbours(value, toward):
    return fetch(value, toward(1)), fetch(value, toward(-1))


def opposite(found, toward, axis):
    size = found[0].shape[axis] // 2
    return (
        fetch(lax.slice_in_dim(found[0], 0, size, axis=axis), toward(1)),
        fetch(lax.slice_in_dim(found[1], size, 2 * size, axis=axis), toward(-1)),
    )


def along_run(values):
    return [values[0]] + [
        fetch(
            values[step],
            lambda y, half, core, run, x, step=step: (y, half, core, run ^ step, x),
        )
        for step in range(1, 4)
    ]


def along_x(values):
    return [values[0]] + [
        fetch(
            values[step],
            lambda y, half, core, run, x, step=step: (y, half, core, run, (x - step) % 4),
        )
        for step in range(1, 4)
    ]


def on_chip(body, place, operands, outputs, scratch=(), flops=0):
    sizes = [v.size * v.dtype.itemsize for v in operands]
    return pl.pallas_call(
        body,
        out_shape=outputs,
        in_specs=[pl.BlockSpec(memory_space=pltpu.SMEM)]
        + [pl.BlockSpec(memory_space=pltpu.VMEM)] * len(operands),
        out_specs=jax.tree.map(lambda _: pl.BlockSpec(memory_space=pltpu.VMEM), outputs),
        scratch_shapes=list(scratch),
        compiler_params=pltpu.CompilerParams(vmem_limit_bytes=40 * 1024 * 1024),
        cost_estimate=pl.CostEstimate(flops=flops, bytes_accessed=sum(sizes), transcendentals=0),
    )(place, *operands)


def shaped(shape, dtype=jnp.bfloat16):
    return jax.ShapeDtypeStruct(shape, dtype)


def aligned(index, size):
    return pl.ds(pl.multiple_of(index * size, size), size)


def stack(target, refs):
    start = 0
    for ref in refs:
        target[start : start + ref.shape[0]] = ref[...]
        start += ref.shape[0]


def gram_body(x, own, other, *refs):
    blocks, outs, (left, right) = refs[:-6], refs[-6:-2], refs[-2:]
    size = own.shape[0] // 2
    for part in range(4):
        rows = (own, other)[part // 2][part % 2 * size : (part % 2 + 1) * size]
        left[aligned((part - x[0]) & 3, size)] = rows
    stack(right, blocks)
    count = right.shape[0]
    width = min(count, 256)
    for start in range(0, count, width):
        stop = min(start + width, count)
        found = lax.dot_general(
            left[...],
            right[start:stop],
            (((1,), (1,)), ((), ())),
            preferred_element_type=jnp.float32,
        ).astype(jnp.bfloat16)
        for step, out in enumerate(outs):
            out[:, start:stop] = found[step * size : (step + 1) * size]


def partial_gram(x, own, other, blocks):
    rows, width = own.shape
    count = sum(block.shape[0] for block in blocks)
    return on_chip(
        gram_body,
        x,
        (own, other, *blocks),
        [shaped((rows // 2, count))] * 4,
        [pltpu.VMEM((2 * rows, width), jnp.bfloat16), pltpu.VMEM((count, width), jnp.bfloat16)],
        4 * rows * width * count,
    )


def quarter(place, rows, cols):
    return aligned(place & 1, rows), aligned(place >> 1, cols)


def split_body(run, *refs):
    parts, outs, summed = refs[:4], refs[4:8], refs[8]
    total = parts[0][...].astype(jnp.float32)
    for part in parts[1:]:
        total = total + part[...].astype(jnp.float32)
    summed[...] = total.astype(jnp.bfloat16)
    for step, out in enumerate(outs):
        rows, cols = quarter(run[0] ^ step, *out.shape)
        out[...] = summed[rows, cols]


def split_sum(run, parts):
    rows, cols = parts[0].shape
    return on_chip(
        split_body,
        run,
        parts,
        [shaped((rows // 2, cols // 2))] * 4,
        [pltpu.VMEM((rows, cols), jnp.bfloat16)],
    )


def strip_body(run, *refs):
    out = refs[4]
    for step, tile in enumerate(refs[:4]):
        rows, cols = quarter(run[0] ^ step, *tile.shape)
        out[rows, cols] = tile[...]


def strip_of(run, tiles):
    rows, cols = tiles[0].shape
    return on_chip(strip_body, run, tiles, shaped((2 * rows, 2 * cols)))


def product_body(strips, partials, x, *refs):
    own, following, first, second, preceding = refs[:strips]
    blocks = refs[strips : -4 - partials]
    before = refs[-4 - partials : -4]
    out, other_out, gram, right = refs[-4:]
    size = own.shape[0]
    for step, strip in ((0, own), (1, following), (3, preceding)):
        gram[aligned((x[0] + step) & 3, size)] = strip[...]
    half = first.shape[1]
    gram[aligned((x[0] + 2) & 3, size), :half] = first[...]
    gram[aligned((x[0] + 2) & 3, size), half:] = second[...]
    stack(right, blocks)
    for place, target in enumerate((out, other_out)):
        rows = gram[place * 2 * size : (place + 1) * 2 * size]
        found = jnp.dot(rows, right[...], preferred_element_type=jnp.float32)
        if partials:
            found = found + before[place][...]
        target[...] = found.astype(target.dtype)


def product(x, strips, blocks, before=()):
    rows, cols = 2 * strips[0].shape[0], strips[0].shape[1]
    width = blocks[0].shape[1]
    last = jnp.bfloat16 if before else jnp.float32
    return on_chip(
        functools.partial(product_body, len(strips), len(before)),
        x,
        (*strips, *blocks, *before),
        [shaped((rows, width), jnp.float32), shaped((rows, width), last)],
        [pltpu.VMEM((2 * rows, cols), jnp.bfloat16), pltpu.VMEM((cols, width), jnp.bfloat16)],
        4 * rows * cols * width,
    )


def total(values):
    summed = values[0].astype(jnp.float32)
    for value in values[1:]:
        summed = summed + value.astype(jnp.float32)
    return summed.astype(jnp.bfloat16)


def local(iterate):
    run = (lax.axis_index("col") // 4).astype(jnp.int32).reshape(1)
    x = (lax.axis_index("col") % 4).astype(jnp.int32).reshape(1)
    total_rows = iterate.shape[0] * lax.axis_size("row")
    total_cols = iterate.shape[1] * lax.axis_size("col")
    narrow = iterate.astype(jnp.bfloat16)
    beside = other_core(narrow)

    found, far = neighbours(narrow, toward_y), other_half(narrow)
    halves, far = ordered((opposite(found, toward_y, 0), far))
    near_blocks = (narrow, found[0], *halves, found[1])
    found = neighbours(far, toward_y)
    near_parts = along_x(partial_gram(x, narrow, beside, near_blocks))
    halves, near_parts = ordered((opposite(found, toward_y, 0), near_parts))
    far_blocks = (far, found[0], *halves, found[1])
    partial, near_parts = ordered((partial_gram(x, narrow, beside, far_blocks), near_parts))
    far_parts = along_x(partial)
    tiles = along_run([total(along_run(split_sum(run, near_parts)))] * 4)
    tiles, far_parts = ordered((tiles, far_parts))
    near_strip = strip_of(run, tiles)
    found, parts = ordered(
        (neighbours(near_strip, toward_x), along_run(split_sum(run, far_parts)))
    )
    halves, tiles = ordered((opposite(found, toward_x, 1), along_run([total(parts)] * 4)))
    near_strips = (near_strip, found[0], *halves, found[1])

    far_strip = strip_of(run, tiles)
    found = neighbours(far_strip, toward_x)
    before, found = ordered((product(x, near_strips, near_blocks), found))
    far_strips = (far_strip, found[0], *opposite(found, toward_x, 1), found[1])
    own, other = product(x, far_strips, far_blocks, before)
    summed = own + other_core(other).astype(jnp.float32)

    inner = (coef_b * narrow.astype(jnp.float32) + coef_c * summed).astype(jnp.bfloat16)
    found, far = neighbours(inner, toward_y), other_half(inner)
    halves, far = ordered((opposite(found, toward_y, 0), far))
    near_blocks = (inner, found[0], *halves, found[1])
    found = neighbours(far, toward_y)
    before, found = ordered((product(x, near_strips, near_blocks), found))
    far_blocks = (far, found[0], *opposite(found, toward_y, 0), found[1])
    own, other = product(x, far_strips, far_blocks, before)
    summed = own + other_core(other).astype(jnp.float32)
    factor = 0.2 * math.sqrt(max(total_rows, total_cols))
    return factor * (coef_a * iterate + summed)


def solution(mesh):
    placed = (P("row", "col"),)
    return jax.shard_map(
        local, mesh=mesh, in_specs=placed, out_specs=P("row", "col"), check_vma=False
    )
```

```python
import functools
import math

import jax
import jax.numpy as jnp
from jax import lax
from jax.experimental import pallas as pl
from jax.experimental.pallas import tpu as pltpu
from jax.sharding import PartitionSpec as P

coef_a = 3.4445
coef_b = -4.775
coef_c = 2.0315

axes = ("row", "col")
ordered = lax.optimization_barrier


def fetch(value, source):
    pairs = []
    for row in range(16):
        for col in range(16):
            y, half, core, run, x = source(row // 4, row // 2 % 2, row % 2, col // 4, col % 4)
            pairs.append((((y * 2 + half) * 2 + core) * 16 + run * 4 + x, row * 16 + col))
    return lax.ppermute(value, axes, pairs)


def other_core(value):
    return fetch(value, lambda y, half, core, run, x: (y, half, 1 - core, run, x))


def other_half(value):
    return fetch(value, lambda y, half, core, run, x: (y, 1 - half, core, run, x))


def toward_y(step):
    return lambda y, half, core, run, x: ((y + step) % 4, half, core, run, x)


def toward_x(step):
    return lambda y, half, core, run, x: (y, half, core, run, (x + step) % 4)


def neighbours(value, toward):
    return fetch(value, toward(1)), fetch(value, toward(-1))


def opposite(found, toward, axis):
    size = found[0].shape[axis] // 2
    return (
        fetch(lax.slice_in_dim(found[0], 0, size, axis=axis), toward(1)),
        fetch(lax.slice_in_dim(found[1], size, 2 * size, axis=axis), toward(-1)),
    )


def along_run(values):
    return [values[0]] + [
        fetch(
            values[step],
            lambda y, half, core, run, x, step=step: (y, half, core, run ^ step, x),
        )
        for step in range(1, 4)
    ]


def along_x(values):
    return [values[0]] + [
        value
        if value is None
        else fetch(
            value, lambda y, half, core, run, x, step=step: (y, half, core, run, (x - step) % 4)
        )
        for step, value in enumerate(values)
        if step
    ]


def on_chip(body, place, operands, outputs, scratch=(), flops=0):
    sizes = [v.size * v.dtype.itemsize for v in operands]
    return pl.pallas_call(
        body,
        out_shape=outputs,
        in_specs=[pl.BlockSpec(memory_space=pltpu.SMEM)]
        + [pl.BlockSpec(memory_space=pltpu.VMEM)] * len(operands),
        out_specs=jax.tree.map(lambda _: pl.BlockSpec(memory_space=pltpu.VMEM), outputs),
        scratch_shapes=list(scratch),
        compiler_params=pltpu.CompilerParams(vmem_limit_bytes=40 * 1024 * 1024),
        cost_estimate=pl.CostEstimate(flops=flops, bytes_accessed=sum(sizes), transcendentals=0),
    )(place, *operands)


def shaped(shape, dtype=jnp.bfloat16):
    return jax.ShapeDtypeStruct(shape, dtype)


def aligned(index, size):
    return pl.ds(pl.multiple_of(index * size, size), size)


def stack(target, refs):
    start = 0
    for ref in refs:
        target[start : start + ref.shape[0]] = ref[...]
        start += ref.shape[0]


def gram_body(x, own, other, *refs):
    blocks, outs, (left, right) = refs[:-6], refs[-6:-2], refs[-2:]
    size = own.shape[0] // 2
    for part in range(4):
        rows = (own, other)[part // 2][part % 2 * size : (part % 2 + 1) * size]
        left[aligned((part - x[0]) & 3, size)] = rows
    stack(right, blocks)
    count = right.shape[0]
    width = min(count, 256)
    for start in range(0, count, width):
        stop = min(start + width, count)
        found = lax.dot_general(
            left[...],
            right[start:stop],
            (((1,), (1,)), ((), ())),
            preferred_element_type=jnp.float32,
        ).astype(jnp.bfloat16)
        for step, out in enumerate(outs):
            out[:, start:stop] = found[step * size : (step + 1) * size]


def partial_gram(x, own, other, blocks):
    rows, width = own.shape
    count = sum(block.shape[0] for block in blocks)
    return on_chip(
        gram_body,
        x,
        (own, other, *blocks),
        [shaped((rows // 2, count))] * 4,
        [pltpu.VMEM((2 * rows, width), jnp.bfloat16), pltpu.VMEM((count, width), jnp.bfloat16)],
        4 * rows * width * count,
    )


def quarter(place, rows, cols):
    return aligned(place & 1, rows), aligned(place >> 1, cols)


def split_body(run, *refs):
    groups, outs, summed = refs[:-5], refs[-5:-1], refs[-1]
    start = 0
    for first in range(0, len(groups), 4):
        found = groups[first][...].astype(jnp.float32)
        for part in groups[first + 1 : first + 4]:
            found = found + part[...].astype(jnp.float32)
        summed[:, start : start + found.shape[1]] = found.astype(jnp.bfloat16)
        start += found.shape[1]
    for step, out in enumerate(outs):
        rows, cols = quarter(run[0] ^ step, *out.shape)
        out[...] = summed[rows, cols]


def split_sum(run, *groups):
    rows, cols = groups[0][0].shape[0], sum(parts[0].shape[1] for parts in groups)
    return on_chip(
        split_body,
        run,
        [part for parts in groups for part in parts],
        [shaped((rows // 2, cols // 2))] * 4,
        [pltpu.VMEM((rows, cols), jnp.bfloat16)],
    )


def strip_body(run, *refs):
    out = refs[4]
    for step, tile in enumerate(refs[:4]):
        rows, cols = quarter(run[0] ^ step, *tile.shape)
        out[rows, cols] = tile[...]


def strip_of(run, tiles):
    rows, cols = tiles[0].shape
    return on_chip(strip_body, run, tiles, shaped((2 * rows, 2 * cols)))


def product_body(strips, partials, x, *refs):
    own, following, first, second, preceding = refs[:strips]
    blocks = refs[strips : -4 - partials]
    before = refs[-4 - partials : -4]
    out, other_out, gram, right = refs[-4:]
    size = own.shape[0]
    for step, strip in ((0, own), (1, following), (3, preceding)):
        gram[aligned((x[0] + step) & 3, size)] = strip[...]
    half = first.shape[1]
    gram[aligned((x[0] + 2) & 3, size), :half] = first[...]
    gram[aligned((x[0] + 2) & 3, size), half:] = second[...]
    stack(right, blocks)
    for place, target in enumerate((out, other_out)):
        rows = gram[place * 2 * size : (place + 1) * 2 * size]
        found = jnp.dot(rows, right[...], preferred_element_type=jnp.float32)
        if partials:
            found = found + before[place][...]
        target[...] = found.astype(target.dtype)


def product(x, strips, blocks, before=()):
    rows, cols = 2 * strips[0].shape[0], strips[0].shape[1]
    width = blocks[0].shape[1]
    last = jnp.bfloat16 if before else jnp.float32
    return on_chip(
        functools.partial(product_body, len(strips), len(before)),
        x,
        (*strips, *blocks, *before),
        [shaped((rows, width), jnp.float32), shaped((rows, width), last)],
        [pltpu.VMEM((2 * rows, cols), jnp.bfloat16), pltpu.VMEM((cols, width), jnp.bfloat16)],
        4 * rows * cols * width,
    )


def total(values):
    summed = values[0].astype(jnp.float32)
    for value in values[1:]:
        summed = summed + value.astype(jnp.float32)
    return summed.astype(jnp.bfloat16)


def local(iterate):
    run = (lax.axis_index("col") // 4).astype(jnp.int32).reshape(1)
    x = (lax.axis_index("col") % 4).astype(jnp.int32).reshape(1)
    total_rows = iterate.shape[0] * lax.axis_size("row")
    total_cols = iterate.shape[1] * lax.axis_size("col")
    narrow = iterate.astype(jnp.bfloat16)
    beside = other_core(narrow)

    def scattered(*blocks):
        return along_x(partial_gram(x, narrow, beside, blocks))

    found, far = neighbours(narrow, toward_y), other_half(narrow)
    halves = opposite(found, toward_y, 0)
    first = partial_gram(x, narrow, beside, found)
    early = along_x([first[0], first[1], None, first[3]])
    second = partial_gram(x, narrow, beside, (narrow, *halves))
    second, far, early = ordered((second, far, early))
    near_blocks = (*found, narrow, *halves)
    second = along_x([*second[:2], jnp.concatenate([first[2], second[2]], axis=1), second[3]])
    found = neighbours(far, toward_y)
    late, second = ordered((found, second))
    second = list(second)
    early = list(early)
    halves = opposite(found, toward_y, 0)
    size = first[0].shape[1]
    across = second[2][:, :size], second[2][:, size:]
    early[2], second[2] = across
    near_parts = along_run(split_sum(run, early, second))
    far_parts = scattered(far, *found, *halves)
    halves, near_parts = ordered((halves, near_parts))
    far_blocks = (far, *late, *halves)

    tiles = along_run([total(near_parts)] * 4)
    parts = split_sum(run, far_parts)
    late, tiles = ordered((parts[0], tiles))
    near_strip = strip_of(run, tiles)
    found = neighbours(near_strip, toward_x)
    tile = total([late, *along_run(parts)[1:]])
    late, found = ordered((tile, found))
    near_strips = (near_strip, found[0], *opposite(found, toward_x, 1), found[1])
    far_strip = strip_of(run, [late, *along_run([tile] * 4)[1:]])
    found = neighbours(far_strip, toward_x)
    before, found = ordered((product(x, near_strips, near_blocks), found))
    far_strips = (far_strip, found[0], *opposite(found, toward_x, 1), found[1])
    own, other = product(x, far_strips, far_blocks, before)
    summed = own + other_core(other).astype(jnp.float32)

    inner = (coef_b * narrow.astype(jnp.float32) + coef_c * summed).astype(jnp.bfloat16)
    found, far = neighbours(inner, toward_y), other_half(inner)
    halves, far = ordered((opposite(found, toward_y, 0), far))
    near_blocks = (*found, inner, *halves)
    found = neighbours(far, toward_y)
    before, found = ordered((product(x, near_strips, near_blocks), found))
    far_blocks = (far, *found, *opposite(found, toward_y, 0))
    own, other = product(x, far_strips, far_blocks, before)
    summed = own + other_core(other).astype(jnp.float32)
    factor = 0.2 * math.sqrt(max(total_rows, total_cols))
    return factor * (coef_a * iterate + summed)


def solution(mesh):
    placed = (P("row", "col"),)
    return jax.shard_map(
        local, mesh=mesh, in_specs=placed, out_specs=P("row", "col"), check_vma=False
    )
```

```python
import functools
import math

import jax
import jax.numpy as jnp
from jax import lax
from jax.experimental import pallas as pl
from jax.experimental.pallas import tpu as pltpu
from jax.sharding import PartitionSpec as P

coef_a = 3.4445
coef_b = -4.775
coef_c = 2.0315

axes = ("row", "col")
ordered = lax.optimization_barrier


def fetch(value, source):
    pairs = []
    for row in range(16):
        for col in range(16):
            y, half, core, run, x = source(row // 4, row // 2 % 2, row % 2, col // 4, col % 4)
            pairs.append((((y * 2 + half) * 2 + core) * 16 + run * 4 + x, row * 16 + col))
    return lax.ppermute(value, axes, pairs)


def other_core(value):
    return fetch(value, lambda y, half, core, run, x: (y, half, 1 - core, run, x))


def other_half(value):
    return fetch(value, lambda y, half, core, run, x: (y, 1 - half, core, run, x))


def toward_y(step):
    return lambda y, half, core, run, x: ((y + step) % 4, half, core, run, x)


def toward_x(step):
    return lambda y, half, core, run, x: (y, half, core, run, (x + step) % 4)


def neighbours(value, toward):
    return fetch(value, toward(1)), fetch(value, toward(-1))


def opposite(found, toward, axis):
    size = found[0].shape[axis] // 2
    return (
        fetch(lax.slice_in_dim(found[0], 0, size, axis=axis), toward(1)),
        fetch(lax.slice_in_dim(found[1], size, 2 * size, axis=axis), toward(-1)),
    )


def along_run(values):
    return [values[0]] + [
        fetch(
            values[step],
            lambda y, half, core, run, x, step=step: (y, half, core, run ^ step, x),
        )
        for step in range(1, 4)
    ]


def along_x(values):
    return [values[0]] + [
        value
        if value is None
        else fetch(
            value, lambda y, half, core, run, x, step=step: (y, half, core, run, (x - step) % 4)
        )
        for step, value in enumerate(values)
        if step
    ]


def on_chip(body, place, operands, outputs, scratch=(), flops=0):
    sizes = [v.size * v.dtype.itemsize for v in operands]
    return pl.pallas_call(
        body,
        out_shape=outputs,
        in_specs=[pl.BlockSpec(memory_space=pltpu.SMEM)]
        + [pl.BlockSpec(memory_space=pltpu.VMEM)] * len(operands),
        out_specs=jax.tree.map(lambda _: pl.BlockSpec(memory_space=pltpu.VMEM), outputs),
        scratch_shapes=list(scratch),
        compiler_params=pltpu.CompilerParams(vmem_limit_bytes=40 * 1024 * 1024),
        cost_estimate=pl.CostEstimate(flops=flops, bytes_accessed=sum(sizes), transcendentals=0),
    )(place, *operands)


def shaped(shape, dtype=jnp.bfloat16):
    return jax.ShapeDtypeStruct(shape, dtype)


def aligned(index, size):
    return pl.ds(pl.multiple_of(index * size, size), size)


def stack(target, refs):
    start = 0
    for ref in refs:
        target[start : start + ref.shape[0]] = ref[...]
        start += ref.shape[0]


def gram_body(x, own, other, *refs):
    blocks, outs, (left, right) = refs[:-6], refs[-6:-2], refs[-2:]
    size = own.shape[0] // 2
    for part in range(4):
        rows = (own, other)[part // 2][part % 2 * size : (part % 2 + 1) * size]
        left[aligned((part - x[0]) & 3, size)] = rows
    stack(right, blocks)
    count = right.shape[0]
    width = min(count, 256)
    for start in range(0, count, width):
        stop = min(start + width, count)
        found = lax.dot_general(
            left[...],
            right[start:stop],
            (((1,), (1,)), ((), ())),
            preferred_element_type=jnp.float32,
        ).astype(jnp.bfloat16)
        for step, out in enumerate(outs):
            out[:, start:stop] = found[step * size : (step + 1) * size]


def partial_gram(x, own, other, blocks):
    rows, width = own.shape
    count = sum(block.shape[0] for block in blocks)
    return on_chip(
        gram_body,
        x,
        (own, other, *blocks),
        [shaped((rows // 2, count))] * 4,
        [pltpu.VMEM((2 * rows, width), jnp.bfloat16), pltpu.VMEM((count, width), jnp.bfloat16)],
        4 * rows * width * count,
    )


def quarter(place, rows, cols):
    return aligned(place & 1, rows), aligned(place >> 1, cols)


def split_body(run, *refs):
    groups, outs, summed = refs[:-5], refs[-5:-1], refs[-1]
    start = 0
    for first in range(0, len(groups), 4):
        found = groups[first][...].astype(jnp.float32)
        for part in groups[first + 1 : first + 4]:
            found = found + part[...].astype(jnp.float32)
        summed[:, start : start + found.shape[1]] = found.astype(jnp.bfloat16)
        start += found.shape[1]
    for step, out in enumerate(outs):
        rows, cols = quarter(run[0] ^ step, *out.shape)
        out[...] = summed[rows, cols]


def split_sum(run, *groups):
    rows, cols = groups[0][0].shape[0], sum(parts[0].shape[1] for parts in groups)
    return on_chip(
        split_body,
        run,
        [part for parts in groups for part in parts],
        [shaped((rows // 2, cols // 2))] * 4,
        [pltpu.VMEM((rows, cols), jnp.bfloat16)],
    )


def strip_body(run, *refs):
    out = refs[4]
    for step, tile in enumerate(refs[:4]):
        rows, cols = quarter(run[0] ^ step, *tile.shape)
        out[rows, cols] = tile[...]


def strip_of(run, tiles):
    rows, cols = tiles[0].shape
    return on_chip(strip_body, run, tiles, shaped((2 * rows, 2 * cols)))


def product_body(strips, partials, x, *refs):
    own, following, first, second, preceding = refs[:strips]
    blocks = refs[strips : -4 - partials]
    before = refs[-4 - partials : -4]
    out, other_out, gram, right = refs[-4:]
    size = own.shape[0]
    for step, strip in ((0, own), (1, following), (3, preceding)):
        gram[aligned((x[0] + step) & 3, size)] = strip[...]
    half = first.shape[1]
    gram[aligned((x[0] + 2) & 3, size), :half] = first[...]
    gram[aligned((x[0] + 2) & 3, size), half:] = second[...]
    stack(right, blocks)
    for place, target in enumerate((out, other_out)):
        rows = gram[place * 2 * size : (place + 1) * 2 * size]
        found = jnp.dot(rows, right[...], preferred_element_type=jnp.float32)
        if partials:
            found = found + before[place][...]
        target[...] = found.astype(target.dtype)


def product(x, strips, blocks, before=()):
    rows, cols = 2 * strips[0].shape[0], strips[0].shape[1]
    width = blocks[0].shape[1]
    last = jnp.bfloat16 if before else jnp.float32
    return on_chip(
        functools.partial(product_body, len(strips), len(before)),
        x,
        (*strips, *blocks, *before),
        [shaped((rows, width), jnp.float32), shaped((rows, width), last)],
        [pltpu.VMEM((2 * rows, cols), jnp.bfloat16), pltpu.VMEM((cols, width), jnp.bfloat16)],
        4 * rows * cols * width,
    )


def total(values):
    summed = values[0].astype(jnp.float32)
    for value in values[1:]:
        summed = summed + value.astype(jnp.float32)
    return summed.astype(jnp.bfloat16)


def local(iterate):
    run = (lax.axis_index("col") // 4).astype(jnp.int32).reshape(1)
    x = (lax.axis_index("col") % 4).astype(jnp.int32).reshape(1)
    total_rows = iterate.shape[0] * lax.axis_size("row")
    total_cols = iterate.shape[1] * lax.axis_size("col")
    narrow = iterate.astype(jnp.bfloat16)
    beside = other_core(narrow)

    def scattered(*blocks):
        return along_x(partial_gram(x, narrow, beside, blocks))

    found, far = neighbours(narrow, toward_y), other_half(narrow)
    halves = opposite(found, toward_y, 0)
    first = partial_gram(x, narrow, beside, found)
    early = along_x([first[0], first[1], None, first[3]])
    second = partial_gram(x, narrow, beside, (narrow, *halves))
    second, far, early = ordered((second, far, early))
    near_blocks = (*found, narrow, *halves)
    second = along_x([*second[:2], jnp.concatenate([first[2], second[2]], axis=1), second[3]])
    found = neighbours(far, toward_y)
    late, second = ordered((found, second))
    second = list(second)
    early = list(early)
    halves = opposite(found, toward_y, 0)
    size = first[0].shape[1]
    across = second[2][:, :size], second[2][:, size:]
    early[2], second[2] = across
    near_parts = along_run(split_sum(run, early, second))
    far_parts = scattered(far, *found, *halves)
    halves, near_parts = ordered((halves, near_parts))
    far_blocks = (far, *late, *halves)

    tiles = along_run([total(near_parts)] * 4)
    parts = split_sum(run, far_parts)
    late, tiles = ordered((parts[0], tiles))
    near_strip = strip_of(run, tiles)
    found = neighbours(near_strip, toward_x)
    tile = total([late, *along_run(parts)[1:]])
    late, found = ordered((tile, found))
    near_strips = (near_strip, found[0], *opposite(found, toward_x, 1), found[1])
    far_strip = strip_of(run, [late, *along_run([tile] * 4)[1:]])
    found = neighbours(far_strip, toward_x)
    halves = opposite(found, toward_x, 1)
    before, kept = ordered((product(x, near_strips, near_blocks), found))
    far_strips = (far_strip, kept[0], *halves, kept[1])
    own, other = product(x, far_strips, far_blocks, before)
    summed = own + other_core(other).astype(jnp.float32)

    inner = (coef_b * narrow.astype(jnp.float32) + coef_c * summed).astype(jnp.bfloat16)
    found, far = neighbours(inner, toward_y), other_half(inner)
    halves, far = ordered((opposite(found, toward_y, 0), far))
    near_blocks = (*found, inner, *halves)
    found = neighbours(far, toward_y)
    before, found = ordered((product(x, near_strips, near_blocks), found))
    far_blocks = (far, *found, *opposite(found, toward_y, 0))
    own, other = product(x, far_strips, far_blocks, before)
    summed = own + other_core(other).astype(jnp.float32)
    factor = 0.2 * math.sqrt(max(total_rows, total_cols))
    return factor * (coef_a * iterate + summed)


def solution(mesh):
    placed = (P("row", "col"),)
    return jax.shard_map(
        local, mesh=mesh, in_specs=placed, out_specs=P("row", "col"), check_vma=False
    )
```
